32 devices in a mesh: row: 4 (over y, core), col: 8 (over z, x).
Axes of the slice: x: 2, y: 2, z: 4, core: 2. Of those that a mesh axis runs over, the one named last changes fastest.
Arguments:
- amplitudes: bfloat16 [8, 8, 4, 128, 128], P('row', 'col'), may hold values from -6 to 6
- cholesky: bfloat16 [8, 8, 10, 128, 128], P('row', 'col'), may hold values from -0.5 to 0.5, as said below
- tile_mask: int32 [8, 8], P('row', 'col'), may hold values 0 or 1
Outputs:
- antisymmetrized: bfloat16 [8, 8, 4, 128, 128], P('row', 'col')
The draws below stay inside these ranges and needn't reach their ends.
Inputs may be any that keep to these rules, and one draw needn't show every extreme that they name: cholesky is symmetric: cholesky[a,c,q,x,u] equals cholesky[c,a,q,u,x].
All inputs are finite; a program needn't handle non-finite values. No bound on the sum of `tile_mask` on one device may be relied on, other than what follows from the above.
Results may differ from the reference program's by a relative error of at most 0.0059.
Values may be sent and summed in bfloat16 or wider, within the bound.
No kernel may reach another device: no remote copies, remote signals or barrier semaphores. Data moves between devices by JAX's collectives and lax.ppermute only.
A program may use at most 128 MiB of HBM per device.

```python
import jax
import jax.numpy as jnp
from jax import lax

TILE = 128
NT = 8
OCC = 2
PAIRS = 4
NQ = 10


def draw_cholesky(key, part):
    array_shape = (NT, NT, NQ, TILE, TILE)
    samples = jnp.clip(jax.random.normal(key, array_shape, jnp.float32), -4.0, 4.0)
    symmetric = (samples + jnp.transpose(samples, (1, 0, 2, 4, 3))) * 0.70710678
    factor = (NT * TILE) ** (-0.5) * (NQ / 2.0) ** (-0.25)
    return (symmetric * factor).astype(jnp.bfloat16)


def plant(values, key, low, top_value):
    longest = values.shape.index(max(values.shape))
    spots = []
    for shift in (0, 1):
        where = [jax.random.randint(jax.random.fold_in(key, axis), (), 0, length) for axis, length in enumerate(values.shape)]
        where[longest] = (where[longest] + shift) % values.shape[longest]
        spots.append(tuple(where))
    return values.at[spots[0]].set(low).at[spots[1]].set(top_value)


def level_of(key, extent, cuts, smallest, top_value):
    loudness, own = 1.0, jax.random.fold_in(key, 6)
    for axis_at, parts in cuts:
        heights = jnp.exp(jax.random.uniform(jax.random.fold_in(own, axis_at), (parts,), jnp.float32, smallest / len(cuts), top_value / len(cuts)))
        loudness = loudness * jnp.repeat(heights, extent[axis_at] // parts).reshape([-1 if axis == axis_at else 1 for axis in range(len(extent))])
    return loudness


def gaussian(own_key, extent, spread, bound, split=(), held_as=jnp.bfloat16):
    array = spread * jax.random.normal(own_key, extent, jnp.float32)
    if split:
        array = array * level_of(own_key, extent, split, -0.22, 0.18)
    return jnp.clip(array, -bound, bound).astype(held_as)


def setup_inputs(seed: int = 0) -> dict:
    arg_keys = jax.random.split(jax.random.key(seed), 4)
    return {
        "amplitudes": gaussian(arg_keys[0], (NT, NT, PAIRS, TILE, TILE), 1.0, 6.0, ((0, 4), (1, 8))),
        "cholesky": draw_cholesky(jax.random.fold_in(arg_keys[3], 71), 0),
        "tile_mask": plant((jax.random.randint(arg_keys[2], (NT, NT), 0, 2) < 1).astype(jnp.int32), jax.random.fold_in(arg_keys[2], 1), 0, 1),
    }


def reference(amplitudes, cholesky, tile_mask):
    weights = cholesky.astype(jnp.float32)
    masked = amplitudes.astype(jnp.float32) * tile_mask.astype(jnp.float32)[:, :, None, None, None]

    def one_column(position):
        column = lax.dynamic_index_in_dim(weights, position, 0, keepdims=False)
        halves = jnp.einsum("cdpuv,dqyv->cpuqy", masked, column)
        halves = lax.optimization_barrier(halves.astype(jnp.bfloat16)).astype(jnp.float32)
        return jnp.einsum("acqxu,cpuqy->apxy", weights, halves)

    ladder = lax.map(one_column, jnp.arange(NT, dtype=jnp.int32))
    ladder = jnp.transpose(ladder, (1, 0, 2, 3, 4))
    rounded = lax.optimization_barrier(ladder.astype(jnp.bfloat16)).astype(jnp.float32)
    mirror = jnp.transpose(rounded, (1, 0, 2, 4, 3)).reshape(NT, NT, OCC, OCC, TILE, TILE)
    mirror = jnp.transpose(mirror, (0, 1, 3, 2, 4, 5)).reshape(NT, NT, PAIRS, TILE, TILE)
    return (rounded - mirror).astype(jnp.bfloat16)
```

```python
import functools
import math

import jax
import jax.numpy as jnp
from jax import lax
from jax.experimental import pallas as pl
from jax.experimental.pallas import tpu as pltpu
from jax.sharding import PartitionSpec as P

ROWS, PLANES, BLOCKS = 4, 4, 10
SLOT_OF = {
    (0, 0): 0, (1, 0): 1, (2, 0): 2, (3, 0): 3, (1, 1): 4,
    (3, 1): 5, (2, 2): 6, (3, 2): 7, (3, 3): 8, (2, 1): 9,
}


def move(value, rule):
    pairs = []
    for r in range(ROWS):
        for z in range(PLANES):
            for x in range(2):
                to = rule(r, z, x)
                if to is not None:
                    pairs.append((r * 2 * PLANES + 2 * z + x, to[0] * 2 * PLANES + 2 * to[1] + to[2]))
    return lax.ppermute(value, ("row", "col"), pairs)


def swap_core(value):
    return move(value, lambda r, z, x: (r ^ 1, z, x))


def swap_y(value):
    return move(value, lambda r, z, x: (r ^ 2, z, x))


def swap_x(value):
    return move(value, lambda r, z, x: (r, z, x ^ 1))


def antisym_kernel(info, own, side, mirror_own, mirror_side, out):
    x = info[0]
    for rr in range(2):
        for cc in range(2):
            for p in range(2):
                tiles = (own, side)[cc]
                mirror = (mirror_own, mirror_side)[rr]
                swapped = jnp.where(x == 0, 1 - p, p)
                here = tiles[rr ^ x, p].astype(jnp.float32)
                there = mirror[cc ^ x, swapped].astype(jnp.float32)
                out[p, pl.ds(rr * 128, 128), pl.ds(cc * 128, 128)] = (here - there.T).astype(jnp.bfloat16)


def halves_kernel(vectors, info, e_ref, ce_ref, xe_ref, cxe_ref, a0, a1, a2, a3, d0, d1, d2, d3, c0, c1, out, col, amp, rowm, col_sem, amp_sem):
    x, core, g = info[0], info[1], info[2]
    col_copies = []
    for half in range(2):
        for t in range(2):
            for rt in range(2):
                n = half * 4 + t * 2 + rt
                slot = g ^ (half + 2 * t)
                dst = col.at[slot, :, pl.ds(pl.multiple_of((rt ^ x) * 128, 128), 128), :]
                for which, srcs in enumerate(((e_ref, ce_ref), (xe_ref, cxe_ref))):
                    copy = pltpu.make_async_copy(srcs[half].at[t, rt], dst, col_sem.at[n])
                    pl.when(core == which)(copy.start)
                col_copies.append(copy)
    slots = [g, g ^ 2, g ^ 1, g ^ 3]
    for m in (0, 2, 1, 3):
        h = g ^ m
        slots.append(jnp.where(h == 0, 7, jnp.where(h == 1, 4, jnp.where(h == 2, 9, 5))))
    slots += [6 + 2 * (g & 1), 8 - 2 * (g & 1)]
    amp_copies = []
    for n, (ref, slot) in enumerate(zip((a0, a2, a1, a3, d0, d2, d1, d3, c0, c1), slots)):
        copy = pltpu.make_async_copy(ref, amp.at[slot], amp_sem.at[n])
        copy.start()
        amp_copies.append(copy)
    for copy in col_copies:
        copy.wait()
    for w in range(PLANES):
        for q in range(vectors):
            rowm[w, pl.ds(q * 128, 128), :] = col[w, q].T
    for copy in amp_copies:
        copy.wait()
    for w in range(PLANES):
        for p in range(2):
            total = None
            for j in range(PLANES):
                if j <= w:
                    term = lax.dot_general(
                        rowm[j], amp[SLOT_OF[w, j], p], (((1,), (1,)), ((), ())), preferred_element_type=jnp.float32
                    )
                    total = term if total is None else total + term
                else:
                    swapped = jnp.where(x == 0, 1 - p, p)
                    term = jnp.dot(rowm[j], amp[SLOT_OF[j, w], swapped], preferred_element_type=jnp.float32)
                    total = -term if total is None else total - term
            total = total.astype(jnp.bfloat16)
            for q in range(vectors):
                out[w, q, pl.ds(p * 128, 128), :] = total[q * 128 : (q + 1) * 128]


def ladder_kernel(vectors, info, *refs):
    own = refs[:4]
    far = refs[4:16]
    halves, out, mat, sem = refs[16:]
    x, core, g = info[0], info[1], info[2]
    copies = []

    def load(src, slot, cc, rt):
        dst = mat.at[slot, :, pl.ds(pl.multiple_of((rt ^ x) * 128, 128), 128), pl.ds(cc * 128, 128)]
        copy = pltpu.make_async_copy(src, dst, sem.at[len(copies)])
        copy.start()
        copies.append(copy)

    for cc in range(2):
        for half in range(2):
            ref = own[cc * 2 + half]
            for t in range(2):
                for rt in range(2):
                    load(ref.at[t, rt], g ^ (half + 2 * t), cc, rt)
    for group in range(3):
        for cc in range(2):
            for half in range(2):
                ref = far[group * 4 + cc * 2 + half]
                for rt in range(2):
                    load(ref.at[rt], 4 + 2 * group + (core ^ half), cc, rt)
    for copy in copies:
        copy.wait()
    for w in range(PLANES):
        def step(q, total):
            for j in range(PLANES):
                if j <= w:
                    total = total + lax.dot_general(
                        halves[j, q], mat[SLOT_OF[w, j], q], (((1,), (1,)), ((), ())), preferred_element_type=jnp.float32
                    )
                else:
                    total = total + jnp.dot(halves[j, q], mat[SLOT_OF[j, w], q], preferred_element_type=jnp.float32)
            return total

        total = jnp.zeros((256, 256), jnp.float32)
        for q in range(vectors):
            total = step(q, total)
        for rr in range(2):
            for p in range(2):
                out[w, rr, p] = total[p * 128 : (p + 1) * 128, rr * 128 : (rr + 1) * 128].T.astype(jnp.bfloat16)


SMEM = pl.BlockSpec(memory_space=pltpu.SMEM)
VMEM = pl.BlockSpec(memory_space=pltpu.VMEM)
ANY = pl.BlockSpec(memory_space=pl.ANY)


def fast_body(amplitudes, cholesky, tile_mask):
    vectors = cholesky.shape[2] // 2
    r, k = lax.axis_index("row"), lax.axis_index("col")
    y, core, z, x = r >> 1, r & 1, k >> 1, k & 1
    g = r ^ z
    info = jnp.stack([x, core, g, y]).astype(jnp.int32)

    factors = cholesky[:, 0]
    kept = lax.dynamic_slice_in_dim(factors, y * vectors, vectors, 1)
    given = lax.dynamic_slice_in_dim(factors, (1 - y) * vectors, vectors, 1)
    e = jnp.stack([kept, swap_y(given)])
    ce = swap_core(e)
    every = jnp.concatenate([e, ce])

    def piece(s):
        m = s ^ g
        return lax.dynamic_index_in_dim(every, (m >> 1) + 2 * (m & 1), 0, keepdims=False)

    far = []
    for by_core in (((0, 1), (2, 1)), ((0, 2), (1, 2)), ((0, 3), (3, 1))):
        s = jnp.where(core == 0, by_core[0][0], by_core[1][0])
        got = move(piece(s), lambda r, z, x: (r, z ^ by_core[r & 1][1], x))
        beside = swap_x(got)
        far += [got, swap_core(got), beside, swap_core(beside)]
    xe = swap_x(e)
    cxe = swap_core(xe)

    masked = jnp.where(tile_mask[:, :, None, None, None] != 0, amplitudes, jnp.bfloat16(0))[:, 0]
    crossed = masked[:, 1:3]
    straight = jnp.stack([masked[:, 0], masked[:, 3]], axis=1)
    own_pairs = jnp.where(x == 0, crossed, straight)
    other_pairs = jnp.where(x == 0, straight, crossed)
    beside = swap_x(other_pairs)
    mirror_own = move(own_pairs, lambda r, z, x: (z, r, x))
    mirror_beside = move(other_pairs, lambda r, z, x: (z, r, x ^ 1))
    a0 = pl.pallas_call(
        antisym_kernel,
        out_shape=jax.ShapeDtypeStruct((2, 256, 256), jnp.bfloat16),
        in_specs=[SMEM] + [VMEM] * 4,
        out_specs=VMEM,
        cost_estimate=pl.CostEstimate(flops=1 << 20, bytes_accessed=3 << 20, transcendentals=0),
    )(info, own_pairs, beside, mirror_own, mirror_beside)
    a2 = swap_y(a0)
    a1, a3 = swap_core(a0), swap_core(a2)
    d0 = move(a0, lambda r, z, x: (r ^ 3, z ^ 2, x) if r ^ z == 1 else (r, z ^ 1, x))
    d2 = swap_y(d0)
    d1, d3 = swap_core(d0), swap_core(d2)
    far2 = move(a0, lambda r, z, x: (r, z ^ 2, x) if r == z else None)
    far3 = move(a0, lambda r, z, x: (r, z ^ 3, x) if r == z else None)
    c0 = jnp.where(g == 2, far2, far3)
    c_other = move(c0, lambda r, z, x: (r ^ 2, z, x) if r ^ z >= 2 else None)
    c0 = jnp.where(g >= 2, c0, c_other)
    c1 = swap_core(c0)

    halves = pl.pallas_call(
        functools.partial(halves_kernel, vectors),
        out_shape=jax.ShapeDtypeStruct((PLANES, vectors, 256, 256), jnp.bfloat16),
        in_specs=[SMEM] + [ANY] * 14,
        out_specs=VMEM,
        scratch_shapes=[
            pltpu.VMEM((PLANES, vectors, 256, 128), jnp.bfloat16),
            pltpu.VMEM((BLOCKS, 2, 256, 256), jnp.bfloat16),
            pltpu.VMEM((PLANES, vectors * 128, 256), jnp.bfloat16),
            pltpu.SemaphoreType.DMA((8,)),
            pltpu.SemaphoreType.DMA((10,)),
        ],
        compiler_params=pltpu.CompilerParams(vmem_limit_bytes=40 << 20),
        cost_estimate=pl.CostEstimate(flops=2700 << 20, bytes_accessed=8 << 20, transcendentals=0),
    )(info, e, ce, xe, cxe, a0, a1, a2, a3, d0, d1, d2, d3, c0, c1)

    partial = pl.pallas_call(
        functools.partial(ladder_kernel, vectors),
        out_shape=jax.ShapeDtypeStruct((PLANES, 2, 2, 128, 128), jnp.bfloat16),
        in_specs=[SMEM] + [ANY] * 16 + [VMEM],
        out_specs=VMEM,
        scratch_shapes=[
            pltpu.VMEM((BLOCKS, vectors, 256, 256), jnp.bfloat16),
            pltpu.SemaphoreType.DMA((40,)),
        ],
        compiler_params=pltpu.CompilerParams(vmem_limit_bytes=40 << 20),
        cost_estimate=pl.CostEstimate(flops=2700 << 20, bytes_accessed=12 << 20, transcendentals=0),
    )(info, e, ce, xe, cxe, *far, halves)

    sums = []
    for m in range(ROWS):
        part = lax.dynamic_index_in_dim(partial, g ^ m, 0, keepdims=False)
        sums.append(move(part, lambda r, z, x, m=m: (r ^ m, z, x ^ (r & 1))).astype(jnp.float32))
    same, other = sums[0] + sums[2], sums[1] + sums[3]
    mine = (x ^ core) == 0
    crossed = jnp.where(mine, same, other)
    straight = jnp.where(mine, other, same)[::-1]
    result = jnp.stack([straight[:, 0], crossed[:, 0], crossed[:, 1], straight[:, 1]], axis=1)
    return result.astype(jnp.bfloat16)[:, None]


def from_partner(value, axis, apart):
    mask = 2**apart
    pairs = [(source, source ^ mask) for source in range(lax.axis_size(axis))]
    return lax.ppermute(value, axis, pairs)


def flip_row(tile_set, bit_pos):
    bit_value = lax.axis_index("row") >> bit_pos & 1
    kept = lax.dynamic_index_in_dim(tile_set, bit_value, 0, keepdims=False)
    outgoing = lax.dynamic_index_in_dim(tile_set, 1 - bit_value, 0, keepdims=False)
    incoming = from_partner(outgoing, "row", bit_pos)
    slot_zero = jnp.where(bit_value == 0, kept, incoming)
    slot_one = jnp.where(bit_value == 0, incoming, kept)
    return jnp.stack([slot_zero, slot_one])


def flip_col(tile_set, bit_pos):
    bit_value = lax.axis_index("col") >> bit_pos & 1
    kept = lax.dynamic_index_in_dim(tile_set, bit_value, 0, keepdims=False)
    outgoing = lax.dynamic_index_in_dim(tile_set, 1 - bit_value, 0, keepdims=False)
    incoming = from_partner(outgoing, "col", bit_pos)
    slot_zero = jnp.where(bit_value == 0, kept, incoming)
    slot_one = jnp.where(bit_value == 0, incoming, kept)
    return jnp.stack([slot_zero, slot_one])


def mirror_cascade(tile_set):
    col_bits = lax.axis_size("col").bit_length() - 1
    tile_set = flip_col(tile_set, 0)
    for bit_pos in range(1, col_bits):
        tile_set = flip_row(tile_set, bit_pos - 1)
        tile_set = flip_col(tile_set, bit_pos)
        tile_set = flip_row(tile_set, bit_pos - 1)
    return tile_set


def general_body(amplitudes, cholesky, tile_mask):
    tile_rows = amplitudes.shape[0]
    pair_count = amplitudes.shape[2]
    tile_edge = amplitudes.shape[3]
    vectors = cholesky.shape[2]
    occupied = math.isqrt(pair_count)
    column = lax.all_gather(cholesky, "row", axis=0, tiled=True)
    column_mats = jnp.transpose(column[:, 0], (0, 2, 1, 3)).reshape(
        column.shape[0], tile_edge, vectors * tile_edge
    )
    amp_block = lax.all_gather(amplitudes, "col", axis=1, tiled=True)
    mask_block = lax.all_gather(tile_mask, "col", axis=1, tiled=True)
    tile_count = amp_block.shape[1]
    masked = amp_block * mask_block.astype(jnp.bfloat16)[:, :, None, None, None]
    masked = masked.reshape(amp_block.shape[0], tile_count, pair_count * tile_edge, tile_edge)
    halves = jnp.einsum("cnmv,nvz->cmz", masked, column_mats, preferred_element_type=jnp.float32)
    halves = halves.astype(jnp.bfloat16).reshape(
        tile_rows, pair_count, tile_edge, vectors, tile_edge
    )
    spread = lax.all_gather(cholesky, "col", axis=1, tiled=True)
    ladder = lax.psum_scatter(
        jnp.einsum("caqux,cpuqy->apxy", spread, halves, preferred_element_type=jnp.float32),
        "row",
        scatter_dimension=0,
        tiled=True,
    )
    rounded = ladder.astype(jnp.bfloat16)
    mirror = mirror_cascade(rounded)
    own_tiles = lax.optimization_barrier(rounded).astype(jnp.float32)
    flipped = mirror.reshape(tile_rows, occupied, occupied, tile_edge, tile_edge)
    flipped = jnp.transpose(flipped, (0, 2, 1, 4, 3)).reshape(
        tile_rows, pair_count, tile_edge, tile_edge
    )
    result_tiles = (own_tiles - flipped.astype(jnp.float32)).astype(jnp.bfloat16)
    return result_tiles.reshape(tile_rows, 1, pair_count, tile_edge, tile_edge)


def body(amplitudes, cholesky, tile_mask):
    rows, cols = lax.axis_size("row"), lax.axis_size("col")
    fits = amplitudes.shape == (2, 1, 4, 128, 128) and cholesky.shape[2] % 2 == 0
    if rows == ROWS and cols == 2 * PLANES and fits:
        return fast_body(amplitudes, cholesky, tile_mask)
    return general_body(amplitudes, cholesky, tile_mask)


def solution(mesh):
    in_specs = (
        P("row", "col", None, None, None),
        P("row", "col", None, None, None),
        P("row", "col"),
    )
    out_specs = P("row", "col", None, None, None)
    return jax.shard_map(body, mesh=mesh, in_specs=in_specs, out_specs=out_specs, check_vma=False)
```

```python
import functools
import math

import jax
import jax.numpy as jnp
from jax import lax
from jax.experimental import pallas as pl
from jax.experimental.pallas import tpu as pltpu
from jax.sharding import PartitionSpec as P

ROWS, PLANES = 4, 4


def move(value, rule):
    pairs = []
    for r in range(ROWS):
        for z in range(PLANES):
            for x in range(2):
                to = rule(r, z, x)
                if to is not None:
                    pairs.append((r * 2 * PLANES + 2 * z + x, to[0] * 2 * PLANES + 2 * to[1] + to[2]))
    return lax.ppermute(value, ("row", "col"), pairs)


def swap_core(value):
    return move(value, lambda r, z, x: (r ^ 1, z, x))


def swap_y(value):
    return move(value, lambda r, z, x: (r ^ 2, z, x))


def swap_x(value):
    return move(value, lambda r, z, x: (r, z, x ^ 1))


def block_kernel(info, *refs):
    x = info[0]
    out = refs[-1]
    for n in range(len(refs) // 2):
        for rr in range(2):
            for cc in range(2):
                for p in range(2):
                    out[n, p, pl.ds(rr * 128, 128), pl.ds(cc * 128, 128)] = refs[2 * n + cc][rr ^ x, p]


def turn_kernel(info, e, ce, xe, cxe, out):
    x, core, g = info[0], info[1], info[2]
    vectors = e.shape[2]
    for half in range(2):
        for t in range(2):
            for rr in range(2):
                for q in range(vectors):
                    tile = jnp.where(core == 0, (e, ce)[half][t, rr ^ x, q], (xe, cxe)[half][t, rr ^ x, q])
                    out[g ^ (half + 2 * t), pl.ds(q * 128, 128), pl.ds(rr * 128, 128)] = tile.T


def halves_kernel(info, rows, own, other, own3, other3, out, after, total):
    x, g = info[0], info[2]
    for n in range(info.shape[0]):
        after[n] = info[n]
    for j in range(PLANES):
        for p in range(2):
            swapped = jnp.where(x == 0, 1 - p, p)
            mirror = None
            for half, blocks in enumerate(((own, other), (own3, other3))[j == 3]):
                for t in range(2):
                    i = g ^ (half + 2 * t)
                    n = 0 if j == 3 else j
                    block = blocks[t, n, p]
                    term = lax.dot_general(rows[j], block, (((1,), (1,)), ((), ())), preferred_element_type=jnp.float32)
                    total[i, p] = term if j == 0 else total[i, p] + term
                    term = jnp.dot(rows[i], blocks[t, n, swapped], preferred_element_type=jnp.float32)
                    mirror = term if mirror is None else mirror + term
            total[j, p] = total[j, p] - mirror
    for w in range(PLANES):
        for p in range(2):
            value = total[w, p].astype(jnp.bfloat16)
            for q in range(out.shape[1]):
                out[w, q, pl.ds(p * 128, 128), :] = value[q * 128 : (q + 1) * 128]


def ladder_terms(x, halves, cases, total):
    vectors = halves.shape[1]
    for i, j, columns in cases:
        direct, mirror = None, None
        for q in range(vectors):
            factor = jnp.concatenate(
                [jnp.concatenate([columns[cc][rr ^ x, q] for cc in range(2)], axis=1) for rr in range(2)], axis=0
            )
            term = lax.dot_general(halves[j, q], factor, (((1,), (1,)), ((), ())), preferred_element_type=jnp.float32)
            direct = term if direct is None else direct + term
            term = jnp.dot(halves[i, q], factor, preferred_element_type=jnp.float32)
            mirror = term if mirror is None else mirror + term
        total[i] = total[i] + direct
        total[j] = total[j] + jnp.where(i == j, jnp.zeros_like(mirror), mirror)


def ladder_own_kernel(info, halves, e, ce, xe, cxe, total):
    x, g = info[0], info[2]
    for w in range(PLANES):
        total[w] = jnp.zeros(total.shape[1:], jnp.float32)
    cases = []
    for half, (own, side) in enumerate(((e, xe), (ce, cxe))):
        for t in range(2):
            cases.append((g ^ (half + 2 * t), 0, (own.at[t], side.at[t])))
    ladder_terms(x, halves, cases, total)


def ladder_far_kernel(info, halves, held, both, both_other, far, far_other, beside, beside_other, out, total):
    x, g = info[0], info[2]
    total[...] = held[...]
    cases = []
    for half, ref in enumerate((both, both_other)):
        cases.append((*by_parity(g, half, (2, 1), (1, 1)), (ref.at[0], ref.at[1])))
    for n, pairs in enumerate((((2, 2), (3, 2)), ((3, 1), (3, 3)))):
        for half, (own, side) in enumerate(((far, beside), (far_other, beside_other))):
            cases.append((*by_parity(g, half, *pairs), (own.at[n], side.at[n])))
    ladder_terms(x, halves, cases, total)
    for w in range(PLANES):
        for rr in range(2):
            for p in range(2):
                tile = total[w, pl.ds(p * 128, 128), pl.ds(rr * 128, 128)]
                out[w, rr, p] = tile.T.astype(jnp.bfloat16)


def by_parity(g, half, even, odd):
    return tuple(jnp.where((g & 1) == half, a, b) for a, b in zip(even, odd))


SMEM = pl.BlockSpec(memory_space=pltpu.SMEM)
VMEM = pl.BlockSpec(memory_space=pltpu.VMEM)


def small_call(kernel, out_shape, *operands):
    specs = [SMEM if value.dtype == jnp.int32 else VMEM for value in operands]
    return pl.pallas_call(
        kernel,
        out_shape=out_shape,
        in_specs=specs,
        out_specs=jax.tree.map(lambda _: VMEM, out_shape),
        compiler_params=pltpu.CompilerParams(vmem_limit_bytes=8 << 20),
        cost_estimate=pl.CostEstimate(flops=1 << 10, bytes_accessed=1 << 10, transcendentals=0),
    )(*operands)


def fast_body(amplitudes, cholesky, tile_mask):
    vectors = cholesky.shape[2] // 2
    r, k = lax.axis_index("row"), lax.axis_index("col")
    y, core, z, x = r >> 1, r & 1, k >> 1, k & 1
    g = r ^ z
    info = jnp.stack([x, core, g, y]).astype(jnp.int32)
    masked = (amplitudes * tile_mask.astype(jnp.bfloat16)[:, :, None, None, None])[:, 0]
    crossed = masked[:, 1:3]
    straight = jnp.stack([masked[:, 0], masked[:, 3]], axis=1)
    own_pairs = jnp.where(x == 0, crossed, straight)
    other_pairs = jnp.where(x == 0, straight, crossed)
    factors = cholesky[:, 0]
    kept = lax.dynamic_slice_in_dim(factors, y * vectors, vectors, 1)
    given = lax.dynamic_slice_in_dim(factors, (1 - y) * vectors, vectors, 1)
    taken = swap_y(given)
    near = [move(own_pairs, lambda r, z, x: (r, z ^ 1, x)), move(other_pairs, lambda r, z, x: (r, z ^ 1, x ^ 1))]
    away = [move(own_pairs, lambda r, z, x: (r, z ^ 2, x)), move(other_pairs, lambda r, z, x: (r, z ^ 2, x ^ 1))]
    *near, others = lax.optimization_barrier((*near, other_pairs))
    side = swap_x(others)
    taken, side, near, away = lax.optimization_barrier((taken, side, near, away))

    e = jnp.stack([kept, taken])
    ce = swap_core(e)
    xe = swap_x(e)
    got1 = move(jnp.where(g <= 1, kept, taken), lambda r, z, x: (r, z ^ 2, x))
    block2 = small_call(block_kernel, jax.ShapeDtypeStruct((1, 2, 256, 256), jnp.bfloat16), info, *away)
    block3 = move(block2, lambda r, z, x: (r, z ^ 1, x))
    trio_shape = jax.ShapeDtypeStruct((3, 2, 256, 256), jnp.bfloat16)
    trio = small_call(block_kernel, trio_shape, info, own_pairs, side, *near, *away)
    across = swap_y(trio)
    piece = jnp.where((g & 1) == 0, jnp.where(g == 0, kept, taken), jnp.where(g == 3, ce[0], ce[1]))
    got2 = move(piece, lambda r, z, x: (r, z ^ 1 if (r ^ z) & 1 else z ^ 3, x))
    ce, xe, got1, block3, across, got2 = lax.optimization_barrier((ce, xe, got1, block3, across, got2))

    n = (g == 0) | (g == 3)
    piece = jnp.stack([jnp.where(n, kept, taken), jnp.where(n, xe[0], xe[1])])
    both = move(piece, lambda r, z, x: (r, z ^ 1, x))
    far = jnp.stack([got1, got2])
    beside = swap_x(far)
    across3 = swap_y(block3)
    cxe = swap_core(xe)
    blocks = jnp.stack([trio, across])
    rows = small_call(
        turn_kernel, jax.ShapeDtypeStruct((PLANES, vectors * 128, 256), jnp.bfloat16), info, e, ce, xe, cxe
    )
    far_other = swap_core(far)
    near3 = jnp.stack([block3, across3])
    halves, info = pl.pallas_call(
        halves_kernel,
        out_shape=(
            jax.ShapeDtypeStruct((PLANES, vectors, 256, 256), jnp.bfloat16),
            jax.ShapeDtypeStruct(info.shape, info.dtype),
        ),
        in_specs=[SMEM] + [VMEM] * 5,
        out_specs=(VMEM, SMEM),
        scratch_shapes=[pltpu.VMEM((PLANES, 2, vectors * 128, 256), jnp.float32)],
        compiler_params=pltpu.CompilerParams(vmem_limit_bytes=16 << 20),
        cost_estimate=pl.CostEstimate(flops=1 << 10, bytes_accessed=1 << 10, transcendentals=0),
    )(info, rows, blocks, swap_core(blocks), near3, swap_core(near3))
    both, beside, info = lax.optimization_barrier((both, beside, info))

    held = pl.pallas_call(
        ladder_own_kernel,
        out_shape=jax.ShapeDtypeStruct((PLANES, 256, 256), jnp.float32),
        in_specs=[SMEM] + [VMEM] * 5,
        out_specs=VMEM,
        compiler_params=pltpu.CompilerParams(vmem_limit_bytes=8 << 20),
        cost_estimate=pl.CostEstimate(flops=1 << 10, bytes_accessed=1 << 10, transcendentals=0),
    )(info, halves, e, ce, xe, cxe)
    partial = pl.pallas_call(
        ladder_far_kernel,
        out_shape=jax.ShapeDtypeStruct((PLANES, 2, 2, 128, 128), jnp.bfloat16),
        in_specs=[SMEM] + [VMEM] * 8,
        out_specs=VMEM,
        scratch_shapes=[pltpu.VMEM((PLANES, 256, 256), jnp.float32)],
        compiler_params=pltpu.CompilerParams(vmem_limit_bytes=8 << 20),
        cost_estimate=pl.CostEstimate(flops=1 << 10, bytes_accessed=1 << 10, transcendentals=0),
    )(info, halves, held, both, swap_core(both), far, far_other, beside, swap_core(beside))

    sums = []
    for m in range(ROWS):
        part = lax.dynamic_index_in_dim(partial, g ^ m, 0, keepdims=False)
        sums.append(move(part, lambda r, z, x, m=m: (r ^ m, z, x ^ (r & 1))).astype(jnp.float32))
    same, other = sums[0] + sums[2], sums[1] + sums[3]
    mine = (x ^ core) == 0
    crossed = jnp.where(mine, same, other)
    straight = jnp.where(mine, other, same)[::-1]
    result = jnp.stack([straight[:, 0], crossed[:, 0], crossed[:, 1], straight[:, 1]], axis=1)
    return result.astype(jnp.bfloat16)[:, None]


def from_partner(value, axis, apart):
    mask = 2**apart
    pairs = [(source, source ^ mask) for source in range(lax.axis_size(axis))]
    return lax.ppermute(value, axis, pairs)


def flip_row(tile_set, bit_pos):
    bit_value = lax.axis_index("row") >> bit_pos & 1
    kept = lax.dynamic_index_in_dim(tile_set, bit_value, 0, keepdims=False)
    outgoing = lax.dynamic_index_in_dim(tile_set, 1 - bit_value, 0, keepdims=False)
    incoming = from_partner(outgoing, "row", bit_pos)
    slot_zero = jnp.where(bit_value == 0, kept, incoming)
    slot_one = jnp.where(bit_value == 0, incoming, kept)
    return jnp.stack([slot_zero, slot_one])


def flip_col(tile_set, bit_pos):
    bit_value = lax.axis_index("col") >> bit_pos & 1
    kept = lax.dynamic_index_in_dim(tile_set, bit_value, 0, keepdims=False)
    outgoing = lax.dynamic_index_in_dim(tile_set, 1 - bit_value, 0, keepdims=False)
    incoming = from_partner(outgoing, "col", bit_pos)
    slot_zero = jnp.where(bit_value == 0, kept, incoming)
    slot_one = jnp.where(bit_value == 0, incoming, kept)
    return jnp.stack([slot_zero, slot_one])


def mirror_cascade(tile_set):
    col_bits = lax.axis_size("col").bit_length() - 1
    tile_set = flip_col(tile_set, 0)
    for bit_pos in range(1, col_bits):
        tile_set = flip_row(tile_set, bit_pos - 1)
        tile_set = flip_col(tile_set, bit_pos)
        tile_set = flip_row(tile_set, bit_pos - 1)
    return tile_set


def general_body(amplitudes, cholesky, tile_mask):
    tile_rows = amplitudes.shape[0]
    pair_count = amplitudes.shape[2]
    tile_edge = amplitudes.shape[3]
    vectors = cholesky.shape[2]
    occupied = math.isqrt(pair_count)
    column = lax.all_gather(cholesky, "row", axis=0, tiled=True)
    column_mats = jnp.transpose(column[:, 0], (0, 2, 1, 3)).reshape(
        column.shape[0], tile_edge, vectors * tile_edge
    )
    amp_block = lax.all_gather(amplitudes, "col", axis=1, tiled=True)
    mask_block = lax.all_gather(tile_mask, "col", axis=1, tiled=True)
    tile_count = amp_block.shape[1]
    masked = amp_block * mask_block.astype(jnp.bfloat16)[:, :, None, None, None]
    masked = masked.reshape(amp_block.shape[0], tile_count, pair_count * tile_edge, tile_edge)
    halves = jnp.einsum("cnmv,nvz->cmz", masked, column_mats, preferred_element_type=jnp.float32)
    halves = halves.astype(jnp.bfloat16).reshape(
        tile_rows, pair_count, tile_edge, vectors, tile_edge
    )
    spread = lax.all_gather(cholesky, "col", axis=1, tiled=True)
    ladder = lax.psum_scatter(
        jnp.einsum("caqux,cpuqy->apxy", spread, halves, preferred_element_type=jnp.float32),
        "row",
        scatter_dimension=0,
        tiled=True,
    )
    rounded = ladder.astype(jnp.bfloat16)
    mirror = mirror_cascade(rounded)
    own_tiles = lax.optimization_barrier(rounded).astype(jnp.float32)
    flipped = mirror.reshape(tile_rows, occupied, occupied, tile_edge, tile_edge)
    flipped = jnp.transpose(flipped, (0, 2, 1, 4, 3)).reshape(
        tile_rows, pair_count, tile_edge, tile_edge
    )
    result_tiles = (own_tiles - flipped.astype(jnp.float32)).astype(jnp.bfloat16)
    return result_tiles.reshape(tile_rows, 1, pair_count, tile_edge, tile_edge)


def body(amplitudes, cholesky, tile_mask):
    rows, cols = lax.axis_size("row"), lax.axis_size("col")
    fits = amplitudes.shape == (2, 1, 4, 128, 128) and cholesky.shape[2] % 2 == 0
    if rows == ROWS and cols == 2 * PLANES and fits:
        return fast_body(amplitudes, cholesky, tile_mask)
    return general_body(amplitudes, cholesky, tile_mask)


def solution(mesh):
    in_specs = (
        P("row", "col", None, None, None),
        P("row", "col", None, None, None),
        P("row", "col"),
    )
    out_specs = P("row", "col", None, None, None)
    return jax.shard_map(body, mesh=mesh, in_specs=in_specs, out_specs=out_specs, check_vma=False)
```

```python
import functools
import math

import jax
import jax.numpy as jnp
from jax import lax
from jax.experimental import pallas as pl
from jax.experimental.pallas import tpu as pltpu
from jax.sharding import PartitionSpec as P

ROWS, PLANES = 4, 4


def move(value, rule):
    pairs = []
    for r in range(ROWS):
        for z in range(PLANES):
            for x in range(2):
                to = rule(r, z, x)
                if to is not None:
                    pairs.append((r * 2 * PLANES + 2 * z + x, to[0] * 2 * PLANES + 2 * to[1] + to[2]))
    return lax.ppermute(value, ("row", "col"), pairs)


def swap_core(value):
    return move(value, lambda r, z, x: (r ^ 1, z, x))


def swap_y(value):
    return move(value, lambda r, z, x: (r ^ 2, z, x))


def swap_x(value):
    return move(value, lambda r, z, x: (r, z, x ^ 1))


def block_kernel(info, *refs):
    x = info[0]
    out = refs[-1]
    for n in range(len(refs) // 2):
        for rr in range(2):
            for cc in range(2):
                for p in range(2):
                    out[n, p, pl.ds(rr * 128, 128), pl.ds(cc * 128, 128)] = refs[2 * n + cc][rr ^ x, p]


def turn_kernel(info, e, ce, xe, cxe, out, blocks):
    x, core, g = info[0], info[1], info[2]
    vectors = e.shape[2]
    for half in range(2):
        for t in range(2):
            slot = g ^ (half + 2 * t)
            for rr in range(2):
                for q in range(vectors):
                    tiles = [ref[t, rr ^ x, q] for ref in ((e, ce)[half], (xe, cxe)[half])]
                    for cc in range(2):
                        blocks[slot, q, pl.ds(rr * 128, 128), pl.ds(cc * 128, 128)] = tiles[cc]
                    tile = jnp.where(core == 0, tiles[0], tiles[1])
                    out[slot, pl.ds(q * 128, 128), pl.ds(rr * 128, 128)] = tile.T


def halves_kernel(info, rows, mine, own, other, own3, other3, out, after, total):
    x, g = info[0], info[2]
    for n in range(info.shape[0]):
        after[n] = info[n]
    for j in range(PLANES):
        for p in range(2):
            swapped = jnp.where(x == 0, 1 - p, p)
            mirror = None
            for half, blocks in enumerate(((own, other), (own3, other3))[j == 3]):
                for t in range(2):
                    i = g ^ (half + 2 * t)
                    n = 0 if j == 3 else j
                    block = blocks[t, n, p]
                    term = lax.dot_general(rows[j], block, (((1,), (1,)), ((), ())), preferred_element_type=jnp.float32)
                    total[i, p] = term if j == 0 else total[i, p] + term
                    term = jnp.dot(rows[i], blocks[t, n, swapped], preferred_element_type=jnp.float32)
                    mirror = term if mirror is None else mirror + term
            total[j, p] = total[j, p] - mirror
    for w in range(PLANES):
        for p in range(2):
            value = total[w, p].astype(jnp.bfloat16)
            for q in range(out.shape[1]):
                out[w, q, pl.ds(p * 128, 128), :] = value[q * 128 : (q + 1) * 128]


def ladder_terms(halves, cases, total):
    vectors = halves.shape[1]
    for i, j, factors in cases:
        direct, mirror = None, None
        for q in range(vectors):
            factor = factors(q)
            term = lax.dot_general(halves[j, q], factor, (((1,), (1,)), ((), ())), preferred_element_type=jnp.float32)
            direct = term if direct is None else direct + term
            term = jnp.dot(halves[i, q], factor, preferred_element_type=jnp.float32)
            mirror = term if mirror is None else mirror + term
        total[i] = total[i] + direct
        total[j] = total[j] + jnp.where(i == j, jnp.zeros_like(mirror), mirror)


def ladder_own_kernel(info, halves, mine, total):
    vectors = halves.shape[1]
    first = None
    for w in range(PLANES):
        direct = None
        for q in range(vectors):
            term = lax.dot_general(
                halves[0, q], mine[w, q], (((1,), (1,)), ((), ())), preferred_element_type=jnp.float32
            )
            direct = term if direct is None else direct + term
            if w:
                first = first + jnp.dot(halves[w, q], mine[w, q], preferred_element_type=jnp.float32)
        if w:
            total[w] = direct
        else:
            first = direct
    total[0] = first


def ladder_far_kernel(info, halves, held, both, both_other, far, far_other, beside, beside_other, out, total):
    x, g = info[0], info[2]
    total[...] = held[...]

    def factors(columns):
        return lambda q: jnp.concatenate(
            [jnp.concatenate([columns[cc][rr ^ x, q] for cc in range(2)], axis=1) for rr in range(2)], axis=0
        )

    cases = []
    for half, ref in enumerate((both, both_other)):
        cases.append((*by_parity(g, half, (2, 1), (1, 1)), factors((ref.at[0], ref.at[1]))))
    for n, pairs in enumerate((((2, 2), (3, 2)), ((3, 1), (3, 3)))):
        for half, (own, side) in enumerate(((far, beside), (far_other, beside_other))):
            cases.append((*by_parity(g, half, *pairs), factors((own.at[n], side.at[n]))))
    ladder_terms(halves, cases, total)
    for w in range(PLANES):
        for rr in range(2):
            for p in range(2):
                tile = total[w, pl.ds(p * 128, 128), pl.ds(rr * 128, 128)]
                out[w, rr, p] = tile.T.astype(jnp.bfloat16)


def by_parity(g, half, even, odd):
    return tuple(jnp.where((g & 1) == half, a, b) for a, b in zip(even, odd))


SMEM = pl.BlockSpec(memory_space=pltpu.SMEM)
VMEM = pl.BlockSpec(memory_space=pltpu.VMEM)


def small_call(kernel, out_shape, *operands):
    specs = [SMEM if value.dtype == jnp.int32 else VMEM for value in operands]
    return pl.pallas_call(
        kernel,
        out_shape=out_shape,
        in_specs=specs,
        out_specs=jax.tree.map(lambda _: VMEM, out_shape),
        compiler_params=pltpu.CompilerParams(vmem_limit_bytes=8 << 20),
        cost_estimate=pl.CostEstimate(flops=1 << 10, bytes_accessed=1 << 10, transcendentals=0),
    )(*operands)


def fast_body(amplitudes, cholesky, tile_mask):
    vectors = cholesky.shape[2] // 2
    r, k = lax.axis_index("row"), lax.axis_index("col")
    y, core, z, x = r >> 1, r & 1, k >> 1, k & 1
    g = r ^ z
    info = jnp.stack([x, core, g, y]).astype(jnp.int32)
    masked = (amplitudes * tile_mask.astype(jnp.bfloat16)[:, :, None, None, None])[:, 0]
    crossed = masked[:, 1:3]
    straight = jnp.stack([masked[:, 0], masked[:, 3]], axis=1)
    own_pairs = jnp.where(x == 0, crossed, straight)
    other_pairs = jnp.where(x == 0, straight, crossed)
    factors = cholesky[:, 0]
    kept = lax.dynamic_slice_in_dim(factors, y * vectors, vectors, 1)
    given = lax.dynamic_slice_in_dim(factors, (1 - y) * vectors, vectors, 1)
    taken = swap_y(given)
    near = [move(own_pairs, lambda r, z, x: (r, z ^ 1, x)), move(other_pairs, lambda r, z, x: (r, z ^ 1, x ^ 1))]
    away = [move(own_pairs, lambda r, z, x: (r, z ^ 2, x)), move(other_pairs, lambda r, z, x: (r, z ^ 2, x ^ 1))]
    *near, others = lax.optimization_barrier((*near, other_pairs))
    side = swap_x(others)
    taken, side, near, away = lax.optimization_barrier((taken, side, near, away))

    e = jnp.stack([kept, taken])
    ce = swap_core(e)
    xe = swap_x(e)
    block2 = small_call(block_kernel, jax.ShapeDtypeStruct((1, 2, 256, 256), jnp.bfloat16), info, *away)
    block3 = move(block2, lambda r, z, x: (r, z ^ 1, x))
    trio_shape = jax.ShapeDtypeStruct((3, 2, 256, 256), jnp.bfloat16)
    trio = small_call(block_kernel, trio_shape, info, own_pairs, side, *near, *away)
    across = swap_y(trio)
    piece1, ce, kept_again, taken_again = (jnp.where(g <= 1, kept, taken), *lax.optimization_barrier((ce, kept, taken)))
    piece2 = jnp.where((g & 1) == 0, jnp.where(g == 0, kept_again, taken_again), jnp.where(g == 3, ce[0], ce[1]))
    got1 = move(piece1, lambda r, z, x: (r, z ^ 2, x))
    got2 = move(piece2, lambda r, z, x: (r, z ^ 1 if (r ^ z) & 1 else z ^ 3, x))
    n = (g == 0) | (g == 3)
    piece = jnp.stack([jnp.where(n, kept, taken), jnp.where(n, xe[0], xe[1])])
    blocks = jnp.stack([trio, across])
    ce, xe, got1, block3, blocks, got2, piece = lax.optimization_barrier((ce, xe, got1, block3, blocks, got2, piece))

    both = move(piece, lambda r, z, x: (r, z ^ 1, x))
    far = jnp.stack([got1, got2])
    beside = swap_x(far)
    across3 = swap_y(block3)
    cxe = swap_core(xe)
    rows, mine = small_call(
        turn_kernel,
        (
            jax.ShapeDtypeStruct((PLANES, vectors * 128, 256), jnp.bfloat16),
            jax.ShapeDtypeStruct((PLANES, vectors, 256, 256), jnp.bfloat16),
        ),
        info, e, ce, xe, cxe,
    )
    far_other = swap_core(far)
    near3 = jnp.stack([block3, across3])
    halves, info = pl.pallas_call(
        halves_kernel,
        out_shape=(
            jax.ShapeDtypeStruct((PLANES, vectors, 256, 256), jnp.bfloat16),
            jax.ShapeDtypeStruct(info.shape, info.dtype),
        ),
        in_specs=[SMEM] + [VMEM] * 6,
        out_specs=(VMEM, SMEM),
        scratch_shapes=[pltpu.VMEM((PLANES, 2, vectors * 128, 256), jnp.float32)],
        compiler_params=pltpu.CompilerParams(vmem_limit_bytes=16 << 20),
        cost_estimate=pl.CostEstimate(flops=1 << 10, bytes_accessed=1 << 10, transcendentals=0),
    )(info, rows, mine, blocks, swap_core(blocks), near3, swap_core(near3))
    both, beside, info = lax.optimization_barrier((both, beside, info))

    held = pl.pallas_call(
        ladder_own_kernel,
        out_shape=jax.ShapeDtypeStruct((PLANES, 256, 256), jnp.float32),
        in_specs=[SMEM] + [VMEM] * 2,
        out_specs=VMEM,
        compiler_params=pltpu.CompilerParams(vmem_limit_bytes=8 << 20),
        cost_estimate=pl.CostEstimate(flops=1 << 10, bytes_accessed=1 << 10, transcendentals=0),
    )(info, halves, mine)
    partial = pl.pallas_call(
        ladder_far_kernel,
        out_shape=jax.ShapeDtypeStruct((PLANES, 2, 2, 128, 128), jnp.bfloat16),
        in_specs=[SMEM] + [VMEM] * 8,
        out_specs=VMEM,
        scratch_shapes=[pltpu.VMEM((PLANES, 256, 256), jnp.float32)],
        compiler_params=pltpu.CompilerParams(vmem_limit_bytes=8 << 20),
        cost_estimate=pl.CostEstimate(flops=1 << 10, bytes_accessed=1 << 10, transcendentals=0),
    )(info, halves, held, both, swap_core(both), far, far_other, beside, swap_core(beside))

    sums = []
    for m in range(ROWS):
        part = lax.dynamic_index_in_dim(partial, g ^ m, 0, keepdims=False)
        sums.append(move(part, lambda r, z, x, m=m: (r ^ m, z, x ^ (r & 1))).astype(jnp.float32))
    same, other = sums[0] + sums[2], sums[1] + sums[3]
    mine = (x ^ core) == 0
    crossed = jnp.where(mine, same, other)
    straight = jnp.where(mine, other, same)[::-1]
    result = jnp.stack([straight[:, 0], crossed[:, 0], crossed[:, 1], straight[:, 1]], axis=1)
    return result.astype(jnp.bfloat16)[:, None]


def from_partner(value, axis, apart):
    mask = 2**apart
    pairs = [(source, source ^ mask) for source in range(lax.axis_size(axis))]
    return lax.ppermute(value, axis, pairs)


def flip_row(tile_set, bit_pos):
    bit_value = lax.axis_index("row") >> bit_pos & 1
    kept = lax.dynamic_index_in_dim(tile_set, bit_value, 0, keepdims=False)
    outgoing = lax.dynamic_index_in_dim(tile_set, 1 - bit_value, 0, keepdims=False)
    incoming = from_partner(outgoing, "row", bit_pos)
    slot_zero = jnp.where(bit_value == 0, kept, incoming)
    slot_one = jnp.where(bit_value == 0, incoming, kept)
    return jnp.stack([slot_zero, slot_one])


def flip_col(tile_set, bit_pos):
    bit_value = lax.axis_index("col") >> bit_pos & 1
    kept = lax.dynamic_index_in_dim(tile_set, bit_value, 0, keepdims=False)
    outgoing = lax.dynamic_index_in_dim(tile_set, 1 - bit_value, 0, keepdims=False)
    incoming = from_partner(outgoing, "col", bit_pos)
    slot_zero = jnp.where(bit_value == 0, kept, incoming)
    slot_one = jnp.where(bit_value == 0, incoming, kept)
    return jnp.stack([slot_zero, slot_one])


def mirror_cascade(tile_set):
    col_bits = lax.axis_size("col").bit_length() - 1
    tile_set = flip_col(tile_set, 0)
    for bit_pos in range(1, col_bits):
        tile_set = flip_row(tile_set, bit_pos - 1)
        tile_set = flip_col(tile_set, bit_pos)
        tile_set = flip_row(tile_set, bit_pos - 1)
    return tile_set


def general_body(amplitudes, cholesky, tile_mask):
    tile_rows = amplitudes.shape[0]
    pair_count = amplitudes.shape[2]
    tile_edge = amplitudes.shape[3]
    vectors = cholesky.shape[2]
    occupied = math.isqrt(pair_count)
    column = lax.all_gather(cholesky, "row", axis=0, tiled=True)
    column_mats = jnp.transpose(column[:, 0], (0, 2, 1, 3)).reshape(
        column.shape[0], tile_edge, vectors * tile_edge
    )
    amp_block = lax.all_gather(amplitudes, "col", axis=1, tiled=True)
    mask_block = lax.all_gather(tile_mask, "col", axis=1, tiled=True)
    tile_count = amp_block.shape[1]
    masked = amp_block * mask_block.astype(jnp.bfloat16)[:, :, None, None, None]
    masked = masked.reshape(amp_block.shape[0], tile_count, pair_count * tile_edge, tile_edge)
    halves = jnp.einsum("cnmv,nvz->cmz", masked, column_mats, preferred_element_type=jnp.float32)
    halves = halves.astype(jnp.bfloat16).reshape(
        tile_rows, pair_count, tile_edge, vectors, tile_edge
    )
    spread = lax.all_gather(cholesky, "col", axis=1, tiled=True)
    ladder = lax.psum_scatter(
        jnp.einsum("caqux,cpuqy->apxy", spread, halves, preferred_element_type=jnp.float32),
        "row",
        scatter_dimension=0,
        tiled=True,
    )
    rounded = ladder.astype(jnp.bfloat16)
    mirror = mirror_cascade(rounded)
    own_tiles = lax.optimization_barrier(rounded).astype(jnp.float32)
    flipped = mirror.reshape(tile_rows, occupied, occupied, tile_edge, tile_edge)
    flipped = jnp.transpose(flipped, (0, 2, 1, 4, 3)).reshape(
        tile_rows, pair_count, tile_edge, tile_edge
    )
    result_tiles = (own_tiles - flipped.astype(jnp.float32)).astype(jnp.bfloat16)
    return result_tiles.reshape(tile_rows, 1, pair_count, tile_edge, tile_edge)


def body(amplitudes, cholesky, tile_mask):
    rows, cols = lax.axis_size("row"), lax.axis_size("col")
    fits = amplitudes.shape == (2, 1, 4, 128, 128) and cholesky.shape[2] % 2 == 0
    if rows == ROWS and cols == 2 * PLANES and fits:
        return fast_body(amplitudes, cholesky, tile_mask)
    return general_body(amplitudes, cholesky, tile_mask)


def solution(mesh):
    in_specs = (
        P("row", "col", None, None, None),
        P("row", "col", None, None, None),
        P("row", "col"),
    )
    out_specs = P("row", "col", None, None, None)
    return jax.shard_map(body, mesh=mesh, in_specs=in_specs, out_specs=out_specs, check_vma=False)
```

```python
import functools
import math

import jax
import jax.numpy as jnp
from jax import lax
from jax.experimental import pallas as pl
from jax.experimental.pallas import tpu as pltpu
from jax.sharding import PartitionSpec as P

ROWS, PLANES = 4, 4


def move(value, rule):
    pairs = []
    for r in range(ROWS):
        for z in range(PLANES):
            for x in range(2):
                to = rule(r, z, x)
                if to is not None:
                    pairs.append((r * 2 * PLANES + 2 * z + x, to[0] * 2 * PLANES + 2 * to[1] + to[2]))
    return lax.ppermute(value, ("row", "col"), pairs)


def swap_core(value):
    return move(value, lambda r, z, x: (r ^ 1, z, x))


def swap_y(value):
    return move(value, lambda r, z, x: (r ^ 2, z, x))


def swap_x(value):
    return move(value, lambda r, z, x: (r, z, x ^ 1))


def block_kernel(info, *refs):
    x = info[0]
    out = refs[-1]
    for n in range(len(refs) // 2):
        for rr in range(2):
            for cc in range(2):
                for p in range(2):
                    out[n, p, pl.ds(rr * 128, 128), pl.ds(cc * 128, 128)] = refs[2 * n + cc][rr ^ x, p]


def turn_kernel(info, e, ce, xe, cxe, out, blocks):
    x, core, g = info[0], info[1], info[2]
    vectors = e.shape[2]
    for half in range(2):
        for t in range(2):
            slot = g ^ (half + 2 * t)
            for rr in range(2):
                for q in range(vectors):
                    tiles = [ref[t, rr ^ x, q] for ref in ((e, ce)[half], (xe, cxe)[half])]
                    for cc in range(2):
                        blocks[slot, q, pl.ds(rr * 128, 128), pl.ds(cc * 128, 128)] = tiles[cc]
                    tile = jnp.where(core == 0, tiles[0], tiles[1])
                    out[slot, pl.ds(q * 128, 128), pl.ds(rr * 128, 128)] = tile.T


def halves_kernel(info, rows, mine, own, other, own3, other3, out, after, total):
    x, g = info[0], info[2]
    for n in range(info.shape[0]):
        after[n] = info[n]
    for j in range(PLANES):
        for p in range(2):
            swapped = jnp.where(x == 0, 1 - p, p)
            mirror = None
            for half, blocks in enumerate(((own, other), (own3, other3))[j == 3]):
                for t in range(2):
                    i = g ^ (half + 2 * t)
                    n = 0 if j == 3 else j
                    block = blocks[t, n, p]
                    term = lax.dot_general(rows[j], block, (((1,), (1,)), ((), ())), preferred_element_type=jnp.float32)
                    total[i, p] = term if j == 0 else total[i, p] + term
                    term = jnp.dot(rows[i], blocks[t, n, swapped], preferred_element_type=jnp.float32)
                    mirror = term if mirror is None else mirror + term
            total[j, p] = total[j, p] - mirror
    for w in range(PLANES):
        for p in range(2):
            value = total[w, p].astype(jnp.bfloat16)
            for q in range(out.shape[1]):
                out[w, q, pl.ds(p * 128, 128), :] = value[q * 128 : (q + 1) * 128]


def ladder_terms(halves, cases, total):
    vectors = halves.shape[1]
    for i, j, factors in cases:
        direct, mirror = None, None
        for q in range(vectors):
            factor = factors(q)
            term = lax.dot_general(halves[j, q], factor, (((1,), (1,)), ((), ())), preferred_element_type=jnp.float32)
            direct = term if direct is None else direct + term
            term = jnp.dot(halves[i, q], factor, preferred_element_type=jnp.float32)
            mirror = term if mirror is None else mirror + term
        total[i] = total[i] + direct
        total[j] = total[j] + jnp.where(i == j, jnp.zeros_like(mirror), mirror)


def ladder_own_kernel(info, halves, mine, total):
    vectors = halves.shape[1]
    first = None
    for w in range(PLANES):
        direct = None
        for q in range(vectors):
            term = lax.dot_general(
                halves[0, q], mine[w, q], (((1,), (1,)), ((), ())), preferred_element_type=jnp.float32
            )
            direct = term if direct is None else direct + term
            if w:
                first = first + jnp.dot(halves[w, q], mine[w, q], preferred_element_type=jnp.float32)
        if w:
            total[w] = direct
        else:
            first = direct
    total[0] = first


def ladder_far_kernel(info, halves, held, both, both_other, far, far_other, beside, beside_other, out, total):
    x, g = info[0], info[2]
    total[...] = held[...]

    def factors(columns):
        return lambda q: jnp.concatenate(
            [jnp.concatenate([columns[cc][rr ^ x, q] for cc in range(2)], axis=1) for rr in range(2)], axis=0
        )

    cases = []
    for half, ref in enumerate((both, both_other)):
        cases.append((*by_parity(g, half, (2, 1), (1, 1)), factors((ref.at[0], ref.at[1]))))
    for n, pairs in enumerate((((2, 2), (3, 2)), ((3, 1), (3, 3)))):
        for half, (own, side) in enumerate(((far, beside), (far_other, beside_other))):
            cases.append((*by_parity(g, half, *pairs), factors((own.at[n], side.at[n]))))
    ladder_terms(halves, cases, total)
    for w in range(PLANES):
        for rr in range(2):
            for p in range(2):
                tile = total[w, pl.ds(p * 128, 128), pl.ds(rr * 128, 128)]
                out[w, rr, p] = tile.astype(jnp.bfloat16).T


def by_parity(g, half, even, odd):
    return tuple(jnp.where((g & 1) == half, a, b) for a, b in zip(even, odd))


SMEM = pl.BlockSpec(memory_space=pltpu.SMEM)
VMEM = pl.BlockSpec(memory_space=pltpu.VMEM)


def small_call(kernel, out_shape, *operands):
    specs = [SMEM if value.dtype == jnp.int32 else VMEM for value in operands]
    return pl.pallas_call(
        kernel,
        out_shape=out_shape,
        in_specs=specs,
        out_specs=jax.tree.map(lambda _: VMEM, out_shape),
        compiler_params=pltpu.CompilerParams(vmem_limit_bytes=8 << 20),
        cost_estimate=pl.CostEstimate(flops=1 << 10, bytes_accessed=1 << 10, transcendentals=0),
    )(*operands)


def fast_body(amplitudes, cholesky, tile_mask):
    vectors = cholesky.shape[2] // 2
    r, k = lax.axis_index("row"), lax.axis_index("col")
    y, core, z, x = r >> 1, r & 1, k >> 1, k & 1
    g = r ^ z
    info = jnp.stack([x, core, g, y]).astype(jnp.int32)
    masked = (amplitudes * tile_mask.astype(jnp.bfloat16)[:, :, None, None, None])[:, 0]
    crossed = masked[:, 1:3]
    straight = jnp.stack([masked[:, 0], masked[:, 3]], axis=1)
    own_pairs = jnp.where(x == 0, crossed, straight)
    other_pairs = jnp.where(x == 0, straight, crossed)
    factors, own_pairs, other_pairs = lax.optimization_barrier((cholesky, own_pairs, other_pairs))
    factors = factors[:, 0]
    kept = lax.dynamic_slice_in_dim(factors, y * vectors, vectors, 1)
    given = lax.dynamic_slice_in_dim(factors, (1 - y) * vectors, vectors, 1)
    taken = swap_y(given)
    away = [move(own_pairs, lambda r, z, x: (r, z ^ 2, x)), move(other_pairs, lambda r, z, x: (r, z ^ 2, x ^ 1))]
    side = swap_x(other_pairs)
    side, own_again, other_again = lax.optimization_barrier((side, own_pairs, other_pairs))
    near = [move(own_again, lambda r, z, x: (r, z ^ 1, x)), move(other_again, lambda r, z, x: (r, z ^ 1, x ^ 1))]
    taken, side, near, away = lax.optimization_barrier((taken, side, near, away))

    e = jnp.stack([kept, taken])
    ce = swap_core(e)
    xe = swap_x(e)
    block2 = small_call(block_kernel, jax.ShapeDtypeStruct((1, 2, 256, 256), jnp.bfloat16), info, *away)
    block3 = move(block2, lambda r, z, x: (r, z ^ 1, x))
    trio_shape = jax.ShapeDtypeStruct((3, 2, 256, 256), jnp.bfloat16)
    trio = small_call(block_kernel, trio_shape, info, own_pairs, side, *near, *away)
    across = swap_y(trio)
    piece1, ce, kept_again, taken_again = (jnp.where(g <= 1, kept, taken), *lax.optimization_barrier((ce, kept, taken)))
    piece2 = jnp.where((g & 1) == 0, jnp.where(g == 0, kept_again, taken_again), jnp.where(g == 3, ce[0], ce[1]))
    got1 = move(piece1, lambda r, z, x: (r, z ^ 2, x))
    got2 = move(piece2, lambda r, z, x: (r, z ^ 1 if (r ^ z) & 1 else z ^ 3, x))
    n = (g == 0) | (g == 3)
    piece = jnp.stack([jnp.where(n, kept, taken), jnp.where(n, xe[0], xe[1])])
    blocks = jnp.stack([trio, across])
    ce, xe, got1, block3, blocks, got2, piece = lax.optimization_barrier((ce, xe, got1, block3, blocks, got2, piece))

    both = move(piece, lambda r, z, x: (r, z ^ 1, x))
    far = jnp.stack([got1, got2])
    beside = swap_x(far)
    across3 = swap_y(block3)
    cxe = swap_core(xe)
    rows, mine = small_call(
        turn_kernel,
        (
            jax.ShapeDtypeStruct((PLANES, vectors * 128, 256), jnp.bfloat16),
            jax.ShapeDtypeStruct((PLANES, vectors, 256, 256), jnp.bfloat16),
        ),
        info, e, ce, xe, cxe,
    )
    far_other = swap_core(far)
    across3, rows, mine = lax.optimization_barrier((across3, rows, mine))
    near3 = jnp.stack([block3, across3])
    halves, info = pl.pallas_call(
        halves_kernel,
        out_shape=(
            jax.ShapeDtypeStruct((PLANES, vectors, 256, 256), jnp.bfloat16),
            jax.ShapeDtypeStruct(info.shape, info.dtype),
        ),
        in_specs=[SMEM] + [VMEM] * 6,
        out_specs=(VMEM, SMEM),
        scratch_shapes=[pltpu.VMEM((PLANES, 2, vectors * 128, 256), jnp.float32)],
        compiler_params=pltpu.CompilerParams(vmem_limit_bytes=16 << 20),
        cost_estimate=pl.CostEstimate(flops=1 << 10, bytes_accessed=1 << 10, transcendentals=0),
    )(info, rows, mine, blocks, swap_core(blocks), near3, swap_core(near3))
    both, beside, info = lax.optimization_barrier((both, beside, info))

    held = pl.pallas_call(
        ladder_own_kernel,
        out_shape=jax.ShapeDtypeStruct((PLANES, 256, 256), jnp.float32),
        in_specs=[SMEM] + [VMEM] * 2,
        out_specs=VMEM,
        compiler_params=pltpu.CompilerParams(vmem_limit_bytes=8 << 20),
        cost_estimate=pl.CostEstimate(flops=1 << 10, bytes_accessed=1 << 10, transcendentals=0),
    )(info, halves, mine)
    partial = pl.pallas_call(
        ladder_far_kernel,
        out_shape=jax.ShapeDtypeStruct((PLANES, 2, 2, 128, 128), jnp.bfloat16),
        in_specs=[SMEM] + [VMEM] * 8,
        out_specs=VMEM,
        scratch_shapes=[pltpu.VMEM((PLANES, 256, 256), jnp.float32)],
        compiler_params=pltpu.CompilerParams(vmem_limit_bytes=8 << 20),
        cost_estimate=pl.CostEstimate(flops=1 << 10, bytes_accessed=1 << 10, transcendentals=0),
    )(info, halves, held, both, swap_core(both), far, far_other, beside, swap_core(beside))

    sums = []
    for m in range(ROWS):
        part = lax.dynamic_index_in_dim(partial, g ^ m, 0, keepdims=False)
        sums.append(move(part, lambda r, z, x, m=m: (r ^ m, z, x ^ (r & 1))).astype(jnp.float32))
    same, other = sums[0] + sums[2], sums[1] + sums[3]
    mine = (x ^ core) == 0
    crossed = jnp.where(mine, same, other)
    straight = jnp.where(mine, other, same)[::-1]
    result = jnp.stack([straight[:, 0], crossed[:, 0], crossed[:, 1], straight[:, 1]], axis=1)
    return result.astype(jnp.bfloat16)[:, None]


def from_partner(value, axis, apart):
    mask = 2**apart
    pairs = [(source, source ^ mask) for source in range(lax.axis_size(axis))]
    return lax.ppermute(value, axis, pairs)


def flip_row(tile_set, bit_pos):
    bit_value = lax.axis_index("row") >> bit_pos & 1
    kept = lax.dynamic_index_in_dim(tile_set, bit_value, 0, keepdims=False)
    outgoing = lax.dynamic_index_in_dim(tile_set, 1 - bit_value, 0, keepdims=False)
    incoming = from_partner(outgoing, "row", bit_pos)
    slot_zero = jnp.where(bit_value == 0, kept, incoming)
    slot_one = jnp.where(bit_value == 0, incoming, kept)
    return jnp.stack([slot_zero, slot_one])


def flip_col(tile_set, bit_pos):
    bit_value = lax.axis_index("col") >> bit_pos & 1
    kept = lax.dynamic_index_in_dim(tile_set, bit_value, 0, keepdims=False)
    outgoing = lax.dynamic_index_in_dim(tile_set, 1 - bit_value, 0, keepdims=False)
    incoming = from_partner(outgoing, "col", bit_pos)
    slot_zero = jnp.where(bit_value == 0, kept, incoming)
    slot_one = jnp.where(bit_value == 0, incoming, kept)
    return jnp.stack([slot_zero, slot_one])


def mirror_cascade(tile_set):
    col_bits = lax.axis_size("col").bit_length() - 1
    tile_set = flip_col(tile_set, 0)
    for bit_pos in range(1, col_bits):
        tile_set = flip_row(tile_set, bit_pos - 1)
        tile_set = flip_col(tile_set, bit_pos)
        tile_set = flip_row(tile_set, bit_pos - 1)
    return tile_set


def general_body(amplitudes, cholesky, tile_mask):
    tile_rows = amplitudes.shape[0]
    pair_count = amplitudes.shape[2]
    tile_edge = amplitudes.shape[3]
    vectors = cholesky.shape[2]
    occupied = math.isqrt(pair_count)
    column = lax.all_gather(cholesky, "row", axis=0, tiled=True)
    column_mats = jnp.transpose(column[:, 0], (0, 2, 1, 3)).reshape(
        column.shape[0], tile_edge, vectors * tile_edge
    )
    amp_block = lax.all_gather(amplitudes, "col", axis=1, tiled=True)
    mask_block = lax.all_gather(tile_mask, "col", axis=1, tiled=True)
    tile_count = amp_block.shape[1]
    masked = amp_block * mask_block.astype(jnp.bfloat16)[:, :, None, None, None]
    masked = masked.reshape(amp_block.shape[0], tile_count, pair_count * tile_edge, tile_edge)
    halves = jnp.einsum("cnmv,nvz->cmz", masked, column_mats, preferred_element_type=jnp.float32)
    halves = halves.astype(jnp.bfloat16).reshape(
        tile_rows, pair_count, tile_edge, vectors, tile_edge
    )
    spread = lax.all_gather(cholesky, "col", axis=1, tiled=True)
    ladder = lax.psum_scatter(
        jnp.einsum("caqux,cpuqy->apxy", spread, halves, preferred_element_type=jnp.float32),
        "row",
        scatter_dimension=0,
        tiled=True,
    )
    rounded = ladder.astype(jnp.bfloat16)
    mirror = mirror_cascade(rounded)
    own_tiles = lax.optimization_barrier(rounded).astype(jnp.float32)
    flipped = mirror.reshape(tile_rows, occupied, occupied, tile_edge, tile_edge)
    flipped = jnp.transpose(flipped, (0, 2, 1, 4, 3)).reshape(
        tile_rows, pair_count, tile_edge, tile_edge
    )
    result_tiles = (own_tiles - flipped.astype(jnp.float32)).astype(jnp.bfloat16)
    return result_tiles.reshape(tile_rows, 1, pair_count, tile_edge, tile_edge)


def body(amplitudes, cholesky, tile_mask):
    rows, cols = lax.axis_size("row"), lax.axis_size("col")
    fits = amplitudes.shape == (2, 1, 4, 128, 128) and cholesky.shape[2] % 2 == 0
    if rows == ROWS and cols == 2 * PLANES and fits:
        return fast_body(amplitudes, cholesky, tile_mask)
    return general_body(amplitudes, cholesky, tile_mask)


def solution(mesh):
    in_specs = (
        P("row", "col", None, None, None),
        P("row", "col", None, None, None),
        P("row", "col"),
    )
    out_specs = P("row", "col", None, None, None)
    return jax.shard_map(body, mesh=mesh, in_specs=in_specs, out_specs=out_specs, check_vma=False)
```

```python
import functools
import math

import jax
import jax.numpy as jnp
from jax import lax
from jax.experimental import pallas as pl
from jax.experimental.pallas import tpu as pltpu
from jax.sharding import PartitionSpec as P

ROWS, PLANES = 4, 4


def move(value, rule):
    pairs = []
    for r in range(ROWS):
        for z in range(PLANES):
            for x in range(2):
                to = rule(r, z, x)
                if to is not None:
                    pairs.append((r * 2 * PLANES + 2 * z + x, to[0] * 2 * PLANES + 2 * to[1] + to[2]))
    return lax.ppermute(value, ("row", "col"), pairs)


def swap_core(value):
    return move(value, lambda r, z, x: (r ^ 1, z, x))


def swap_y(value):
    return move(value, lambda r, z, x: (r ^ 2, z, x))


def swap_x(value):
    return move(value, lambda r, z, x: (r, z, x ^ 1))


def block_kernel(info, *refs):
    x = info[0]
    out = refs[-1]
    for n in range(len(refs) // 2):
        for rr in range(2):
            for cc in range(2):
                for p in range(2):
                    out[n, p, pl.ds(rr * 128, 128), pl.ds(cc * 128, 128)] = refs[2 * n + cc][rr ^ x, p]


def turn_kernel(info, e, ce, xe, cxe, out, blocks):
    x, core, g = info[0], info[1], info[2]
    vectors = e.shape[2]
    for half in range(2):
        for t in range(2):
            slot = g ^ (half + 2 * t)
            for rr in range(2):
                for q in range(vectors):
                    tiles = [ref[t, rr ^ x, q] for ref in ((e, ce)[half], (xe, cxe)[half])]
                    for cc in range(2):
                        blocks[slot, q, pl.ds(rr * 128, 128), pl.ds(cc * 128, 128)] = tiles[cc]
                    tile = jnp.where(core == 0, tiles[0], tiles[1])
                    out[slot, pl.ds(q * 128, 128), pl.ds(rr * 128, 128)] = tile.T


def halves_kernel(info, rows, mine, own, other, own3, other3, out, after, total):
    x, g = info[0], info[2]
    for n in range(info.shape[0]):
        after[n] = info[n]
    for j in range(PLANES):
        for p in range(2):
            swapped = jnp.where(x == 0, 1 - p, p)
            mirror = None
            for half, blocks in enumerate(((own, other), (own3, other3))[j == 3]):
                for t in range(2):
                    i = g ^ (half + 2 * t)
                    n = 0 if j == 3 else j
                    block = blocks[t, n, p]
                    term = lax.dot_general(rows[j], block, (((1,), (1,)), ((), ())), preferred_element_type=jnp.float32)
                    total[i, p] = term if j == 0 else total[i, p] + term
                    term = jnp.dot(rows[i], blocks[t, n, swapped], preferred_element_type=jnp.float32)
                    mirror = term if mirror is None else mirror + term
            total[j, p] = total[j, p] - mirror
    for w in range(PLANES):
        for p in range(2):
            value = total[w, p].astype(jnp.bfloat16)
            for q in range(out.shape[1]):
                out[w, q, pl.ds(p * 128, 128), :] = value[q * 128 : (q + 1) * 128]


def ladder_terms(halves, cases, total):
    vectors = halves.shape[1]
    for i, j, factors in cases:
        direct, mirror = None, None
        for q in range(vectors):
            factor = factors(q)
            term = lax.dot_general(halves[j, q], factor, (((1,), (1,)), ((), ())), preferred_element_type=jnp.float32)
            direct = term if direct is None else direct + term
            term = jnp.dot(halves[i, q], factor, preferred_element_type=jnp.float32)
            mirror = term if mirror is None else mirror + term
        total[i] = total[i] + direct
        total[j] = total[j] + jnp.where(i == j, jnp.zeros_like(mirror), mirror)


def ladder_own_kernel(info, halves, mine, total):
    vectors = halves.shape[1]
    first = None
    for w in range(PLANES):
        direct = None
        for q in range(vectors):
            term = lax.dot_general(
                halves[0, q], mine[w, q], (((1,), (1,)), ((), ())), preferred_element_type=jnp.float32
            )
            direct = term if direct is None else direct + term
            if w:
                first = first + jnp.dot(halves[w, q], mine[w, q], preferred_element_type=jnp.float32)
        if w:
            total[w] = direct
        else:
            first = direct
    total[0] = first


def ladder_far_kernel(info, halves, held, both, both_other, far, far_other, beside, beside_other, out, total):
    x, g = info[0], info[2]
    total[...] = held[...]

    def factors(columns):
        return lambda q: jnp.concatenate(
            [jnp.concatenate([columns[cc][rr ^ x, q] for cc in range(2)], axis=1) for rr in range(2)], axis=0
        )

    cases = []
    for half, ref in enumerate((both, both_other)):
        cases.append((*by_parity(g, half, (2, 1), (1, 1)), factors((ref.at[0], ref.at[1]))))
    for n, pairs in enumerate((((2, 2), (3, 2)), ((3, 1), (3, 3)))):
        for half, (own, side) in enumerate(((far, beside), (far_other, beside_other))):
            cases.append((*by_parity(g, half, *pairs), factors((own.at[n], side.at[n]))))
    ladder_terms(halves, cases, total)
    for w in range(PLANES):
        for rr in range(2):
            for p in range(2):
                tile = total[w, pl.ds(p * 128, 128), pl.ds(rr * 128, 128)]
                out[w, rr, p] = tile.astype(jnp.bfloat16).T


def by_parity(g, half, even, odd):
    return tuple(jnp.where((g & 1) == half, a, b) for a, b in zip(even, odd))


SMEM = pl.BlockSpec(memory_space=pltpu.SMEM)
VMEM = pl.BlockSpec(memory_space=pltpu.VMEM)


def small_call(kernel, out_shape, *operands):
    specs = [SMEM if value.dtype == jnp.int32 else VMEM for value in operands]
    return pl.pallas_call(
        kernel,
        out_shape=out_shape,
        in_specs=specs,
        out_specs=jax.tree.map(lambda _: VMEM, out_shape),
        compiler_params=pltpu.CompilerParams(vmem_limit_bytes=8 << 20),
        cost_estimate=pl.CostEstimate(flops=1 << 10, bytes_accessed=1 << 10, transcendentals=0),
    )(*operands)


def fast_body(amplitudes, cholesky, tile_mask):
    vectors = cholesky.shape[2] // 2
    r, k = lax.axis_index("row"), lax.axis_index("col")
    y, core, z, x = r >> 1, r & 1, k >> 1, k & 1
    g = r ^ z
    info = jnp.stack([x, core, g, y]).astype(jnp.int32)
    masked = (amplitudes * tile_mask.astype(jnp.bfloat16)[:, :, None, None, None])[:, 0]
    crossed = masked[:, 1:3]
    straight = jnp.stack([masked[:, 0], masked[:, 3]], axis=1)
    own_pairs = jnp.where(x == 0, crossed, straight)
    other_pairs = jnp.where(x == 0, straight, crossed)
    factors, own_pairs, other_pairs = lax.optimization_barrier((cholesky, own_pairs, other_pairs))
    factors = factors[:, 0]
    kept = lax.dynamic_slice_in_dim(factors, y * vectors, vectors, 1)
    given = lax.dynamic_slice_in_dim(factors, (1 - y) * vectors, vectors, 1)
    taken = swap_y(given)
    away = [move(own_pairs, lambda r, z, x: (r, z ^ 2, x)), move(other_pairs, lambda r, z, x: (r, z ^ 2, x ^ 1))]
    side = swap_x(other_pairs)
    side, own_again, other_again = lax.optimization_barrier((side, own_pairs, other_pairs))
    near = [move(own_again, lambda r, z, x: (r, z ^ 1, x)), move(other_again, lambda r, z, x: (r, z ^ 1, x ^ 1))]
    taken, side, near, away = lax.optimization_barrier((taken, side, near, away))

    e = jnp.stack([kept, taken])
    ce = swap_core(e)
    xe = swap_x(e)
    block2 = small_call(block_kernel, jax.ShapeDtypeStruct((1, 2, 256, 256), jnp.bfloat16), info, *away)
    block3 = move(block2, lambda r, z, x: (r, z ^ 1, x))
    trio_shape = jax.ShapeDtypeStruct((3, 2, 256, 256), jnp.bfloat16)
    trio = small_call(block_kernel, trio_shape, info, own_pairs, side, *near, *away)
    across = swap_y(trio)
    piece1, ce, kept_again, taken_again = (jnp.where(g <= 1, kept, taken), *lax.optimization_barrier((ce, kept, taken)))
    piece2 = jnp.where((g & 1) == 0, jnp.where(g == 0, kept_again, taken_again), jnp.where(g == 3, ce[0], ce[1]))
    got1 = move(piece1, lambda r, z, x: (r, z ^ 2, x))
    got2 = move(piece2, lambda r, z, x: (r, z ^ 1 if (r ^ z) & 1 else z ^ 3, x))
    n = (g == 0) | (g == 3)
    piece = jnp.stack([jnp.where(n, kept, taken), jnp.where(n, xe[0], xe[1])])
    blocks = jnp.stack([trio, across])
    ce, xe, got1, block3, blocks, got2, piece = lax.optimization_barrier((ce, xe, got1, block3, blocks, got2, piece))

    both = move(piece, lambda r, z, x: (r, z ^ 1, x))
    far = jnp.stack([got1, got2])
    beside = swap_x(far)
    across3 = swap_y(block3)
    cxe = swap_core(xe)
    rows, mine = small_call(
        turn_kernel,
        (
            jax.ShapeDtypeStruct((PLANES, vectors * 128, 256), jnp.bfloat16),
            jax.ShapeDtypeStruct((PLANES, vectors, 256, 256), jnp.bfloat16),
        ),
        info, e, ce, xe, cxe,
    )
    far_other = swap_core(far)
    across3, rows, mine = lax.optimization_barrier((across3, rows, mine))
    near3 = jnp.stack([block3, across3])
    halves, info = pl.pallas_call(
        halves_kernel,
        out_shape=(
            jax.ShapeDtypeStruct((PLANES, vectors, 256, 256), jnp.bfloat16),
            jax.ShapeDtypeStruct(info.shape, info.dtype),
        ),
        in_specs=[SMEM] + [VMEM] * 6,
        out_specs=(VMEM, SMEM),
        scratch_shapes=[pltpu.VMEM((PLANES, 2, vectors * 128, 256), jnp.float32)],
        compiler_params=pltpu.CompilerParams(vmem_limit_bytes=16 << 20),
        cost_estimate=pl.CostEstimate(flops=1 << 10, bytes_accessed=1 << 10, transcendentals=0),
    )(info, rows, mine, blocks, swap_core(blocks), near3, swap_core(near3))
    both, beside, info = lax.optimization_barrier((both, beside, info))

    held = pl.pallas_call(
        ladder_own_kernel,
        out_shape=jax.ShapeDtypeStruct((PLANES, 256, 256), jnp.float32),
        in_specs=[SMEM] + [VMEM] * 2,
        out_specs=VMEM,
        compiler_params=pltpu.CompilerParams(vmem_limit_bytes=8 << 20),
        cost_estimate=pl.CostEstimate(flops=1 << 10, bytes_accessed=1 << 10, transcendentals=0),
    )(info, halves, mine)
    partial = pl.pallas_call(
        ladder_far_kernel,
        out_shape=jax.ShapeDtypeStruct((PLANES, 2, 2, 128, 128), jnp.bfloat16),
        in_specs=[SMEM] + [VMEM] * 8,
        out_specs=VMEM,
        scratch_shapes=[pltpu.VMEM((PLANES, 256, 256), jnp.float32)],
        compiler_params=pltpu.CompilerParams(vmem_limit_bytes=8 << 20),
        cost_estimate=pl.CostEstimate(flops=1 << 10, bytes_accessed=1 << 10, transcendentals=0),
    )(info, halves, held, both, swap_core(both), far, far_other, beside, swap_core(beside))

    sums = []
    for m in reversed(range(ROWS)):
        part = lax.dynamic_index_in_dim(partial, g ^ m, 0, keepdims=False)
        sums.append(move(part, lambda r, z, x, m=m: (r ^ m, z, x ^ (r & 1))).astype(jnp.float32))
    same, other = sums[3] + sums[1], sums[2] + sums[0]
    mine = (x ^ core) == 0
    crossed = jnp.where(mine, same, other)
    straight = jnp.where(mine, other, same)[::-1]
    result = jnp.stack([straight[:, 0], crossed[:, 0], crossed[:, 1], straight[:, 1]], axis=1)
    return result.astype(jnp.bfloat16)[:, None]


def from_partner(value, axis, apart):
    mask = 2**apart
    pairs = [(source, source ^ mask) for source in range(lax.axis_size(axis))]
    return lax.ppermute(value, axis, pairs)


def flip_row(tile_set, bit_pos):
    bit_value = lax.axis_index("row") >> bit_pos & 1
    kept = lax.dynamic_index_in_dim(tile_set, bit_value, 0, keepdims=False)
    outgoing = lax.dynamic_index_in_dim(tile_set, 1 - bit_value, 0, keepdims=False)
    incoming = from_partner(outgoing, "row", bit_pos)
    slot_zero = jnp.where(bit_value == 0, kept, incoming)
    slot_one = jnp.where(bit_value == 0, incoming, kept)
    return jnp.stack([slot_zero, slot_one])


def flip_col(tile_set, bit_pos):
    bit_value = lax.axis_index("col") >> bit_pos & 1
    kept = lax.dynamic_index_in_dim(tile_set, bit_value, 0, keepdims=False)
    outgoing = lax.dynamic_index_in_dim(tile_set, 1 - bit_value, 0, keepdims=False)
    incoming = from_partner(outgoing, "col", bit_pos)
    slot_zero = jnp.where(bit_value == 0, kept, incoming)
    slot_one = jnp.where(bit_value == 0, incoming, kept)
    return jnp.stack([slot_zero, slot_one])


def mirror_cascade(tile_set):
    col_bits = lax.axis_size("col").bit_length() - 1
    tile_set = flip_col(tile_set, 0)
    for bit_pos in range(1, col_bits):
        tile_set = flip_row(tile_set, bit_pos - 1)
        tile_set = flip_col(tile_set, bit_pos)
        tile_set = flip_row(tile_set, bit_pos - 1)
    return tile_set


def general_body(amplitudes, cholesky, tile_mask):
    tile_rows = amplitudes.shape[0]
    pair_count = amplitudes.shape[2]
    tile_edge = amplitudes.shape[3]
    vectors = cholesky.shape[2]
    occupied = math.isqrt(pair_count)
    column = lax.all_gather(cholesky, "row", axis=0, tiled=True)
    column_mats = jnp.transpose(column[:, 0], (0, 2, 1, 3)).reshape(
        column.shape[0], tile_edge, vectors * tile_edge
    )
    amp_block = lax.all_gather(amplitudes, "col", axis=1, tiled=True)
    mask_block = lax.all_gather(tile_mask, "col", axis=1, tiled=True)
    tile_count = amp_block.shape[1]
    masked = amp_block * mask_block.astype(jnp.bfloat16)[:, :, None, None, None]
    masked = masked.reshape(amp_block.shape[0], tile_count, pair_count * tile_edge, tile_edge)
    halves = jnp.einsum("cnmv,nvz->cmz", masked, column_mats, preferred_element_type=jnp.float32)
    halves = halves.astype(jnp.bfloat16).reshape(
        tile_rows, pair_count, tile_edge, vectors, tile_edge
    )
    spread = lax.all_gather(cholesky, "col", axis=1, tiled=True)
    ladder = lax.psum_scatter(
        jnp.einsum("caqux,cpuqy->apxy", spread, halves, preferred_element_type=jnp.float32),
        "row",
        scatter_dimension=0,
        tiled=True,
    )
    rounded = ladder.astype(jnp.bfloat16)
    mirror = mirror_cascade(rounded)
    own_tiles = lax.optimization_barrier(rounded).astype(jnp.float32)
    flipped = mirror.reshape(tile_rows, occupied, occupied, tile_edge, tile_edge)
    flipped = jnp.transpose(flipped, (0, 2, 1, 4, 3)).reshape(
        tile_rows, pair_count, tile_edge, tile_edge
    )
    result_tiles = (own_tiles - flipped.astype(jnp.float32)).astype(jnp.bfloat16)
    return result_tiles.reshape(tile_rows, 1, pair_count, tile_edge, tile_edge)


def body(amplitudes, cholesky, tile_mask):
    rows, cols = lax.axis_size("row"), lax.axis_size("col")
    fits = amplitudes.shape == (2, 1, 4, 128, 128) and cholesky.shape[2] % 2 == 0
    if rows == ROWS and cols == 2 * PLANES and fits:
        return fast_body(amplitudes, cholesky, tile_mask)
    return general_body(amplitudes, cholesky, tile_mask)


def solution(mesh):
    in_specs = (
        P("row", "col", None, None, None),
        P("row", "col", None, None, None),
        P("row", "col"),
    )
    out_specs = P("row", "col", None, None, None)
    return jax.shard_map(body, mesh=mesh, in_specs=in_specs, out_specs=out_specs, check_vma=False)
```
